32 devices in a mesh: group: 2 (over y), expert: 8 (over z, x), tensor: 2 (over core).
Axes of the slice: x: 2, y: 2, z: 4, core: 2. Of those that a mesh axis runs over, the one named last changes fastest.
Arguments:
- tokens: bfloat16 [2048, 4096], P(('group', 'expert'), 'tensor'), parts along dimension 0, may hold values from -6 to 6
- expert_ids: int32 [2048, 2], P(('group', 'expert')), parts along dimension 0, may hold values from 0 to 7, all different within a row; in each aligned block of 128 rows (0 to 127, 128 to 255, ...) at most 40 rows name the same one
- gate_scores: float32 [2048, 2], P(('group', 'expert')), parts along dimension 0, may hold values from 0.05 to 1
- gate_weight: bfloat16 [8, 4096, 768], P('expert', 'tensor'), may hold values from -0.09375 to 0.09375
- up_weight: bfloat16 [8, 4096, 768], P('expert', 'tensor'), may hold values from -0.09375 to 0.09375
- down_weight: bfloat16 [8, 768, 4096], P('expert', None, 'tensor'), may hold values from -0.21875 to 0.21875
Outputs:
- combined: bfloat16 [2048, 4096], P(('group', 'expert'), 'tensor'), parts along dimension 0
The draws below stay inside these ranges and needn't reach their ends.
There are 2 independent parts, one for each index of `group`. The reference program is written for one: setup_inputs(seed, part) draws one part's arguments, and reference() takes and returns one part's arrays. A program takes and returns all parts, laid end to end along the dimension named above; an argument that names none is the same for every part. Nothing has to cross between parts.
Inputs may be any that keep to these rules, and one draw needn't show every extreme that they name: `expert_ids`: the 2 experts of a token differ. Within each aligned block of 128 rows (the rows of one index of expert), no expert is named by more than 40 rows, a bound that some block reaches.
All inputs are finite; a program needn't handle non-finite values.
Results may differ from the reference program's by a relative error of at most 0.0058.
Values may be sent and summed in bfloat16 or wider, within the bound.
A program may use at most 128 MiB of HBM per device.

```python
import math
import jax
import jax.numpy as jnp
import numpy as np
from jax import lax

D = 4096
HID = 768
TOK_DEV = 128
EXPERTS = 8
TOP = 2
CAP = 40
TOKENS = 1024
N_EXPERT = 8


def level_of(stream_key, extent, shards, smallest, largest):
    def one(dim, blocks):
        draws = jax.random.uniform(jax.random.fold_in(jax.random.fold_in(stream_key, 6), dim), (blocks,), jnp.float32, smallest / len(shards), largest / len(shards))
        return jnp.repeat(jnp.exp(draws), extent[dim] // blocks).reshape((-1,) + (1,) * (len(extent) - dim - 1))

    gain = one(*shards[0])
    for cut in shards[1:]:
        gain = gain * one(*cut)
    return gain


def deal_out(rng, own, number, rows, count, top, limit, skew):
    order = jax.random.permutation(rng, count)
    heavy_load, ordinary = portions_of(count, rows * top, limit, skew, True), portions_of(count, rows * top, limit, skew, False)
    places = jnp.arange(count)

    def named(tallies, turn):
        used = int((tallies > 0).sum())
        fixed = max(1, used // 4)
        shifted = fixed + (places - fixed + turn * (used - fixed)) % max(1, count - fixed)
        return jnp.zeros((count,), jnp.int32).at[order[jnp.where(places < fixed, places, shifted)]].set(jnp.asarray(tallies, jnp.int32))

    tallies = jnp.where(number % 4 == 0, named(heavy_load, number // 4), named(ordinary, number - number // 4 - 1))
    mixed = jax.random.permutation(jax.random.fold_in(own, 3), count)
    giver, taker = mixed[0:count // 2 * 2:2], mixed[1:count // 2 * 2:2]
    room = jnp.minimum(tallies[giver] - 1, limit - tallies[taker]) // 2
    room = jnp.where((giver == order[0]) | (taker == order[0]) | (tallies[taker] == 0), 0, jnp.maximum(room, 0))
    shifted = jax.random.randint(jax.random.fold_in(own, 4), (count // 2,), 0, 1 << 20) % (room + 1)
    tallies = tallies.at[giver].add(-shifted).at[taker].add(shifted)
    items = jnp.searchsorted(jnp.cumsum(tallies), jnp.arange(rows * top), side="right").astype(jnp.int32)
    table = items.reshape(top, rows).T
    table = table[jax.random.permutation(jax.random.fold_in(own, 1), rows)]
    turn = jax.random.randint(jax.random.fold_in(own, 2), (rows, 1), 0, top)
    return jnp.take_along_axis(table, (jnp.arange(top)[None, :] + turn) % top, axis=1)


def portions_of(amount, total, bound, skew, full):
    loads = [(1 << 20) // math.isqrt(grade ** skew) + 1 for grade in range(1, amount + 1)]
    largest = bound if full else min(bound, max(-(-total // amount), total * loads[0] // sum(loads)))
    least = 1 if total - largest >= amount - 1 else 0
    holding, surplus = [largest] + [least] * (amount - 1), total - largest - least * (amount - 1)
    while surplus > 0:
        free = [i for i in range(1, amount) if holding[i] < largest] or [i for i in range(1, amount) if holding[i] < bound]
        whole, left = sum([loads[i] for i in free]), surplus
        for i in free:
            extra = min(bound - holding[i], max(1, left * loads[i] // whole), surplus)
            holding[i] = holding[i] + extra
            surplus = surplus - extra
    return np.array(holding)


def bell_draw(stream_key, shape, scale, limit, shards=(), kind=jnp.bfloat16):
    entries = scale * jax.random.normal(stream_key, shape, jnp.float32)
    if shards:
        entries = entries * level_of(stream_key, shape, shards, -0.22, 0.18)
    return jnp.clip(entries, -limit, limit).astype(kind)


def setup_inputs(seed: int = 0, part: int = 0) -> dict:
    key_of = jax.random.split(jax.random.key(seed), 7)
    part_splits = jax.random.split(jax.random.fold_in(key_of[6], part), 7)
    tokens = bell_draw(part_splits[0], (TOKENS, D), 1.0, 6.0, ((0, 8), (1, 2)))
    expert_ids_keys = jax.random.split(jax.random.fold_in(part_splits[1], 1), TOKENS // TOK_DEV)
    expert_ids_turns = jax.random.permutation(jax.random.fold_in(part_splits[1], 3), TOKENS // TOK_DEV)
    expert_ids = jax.vmap(lambda own, number: deal_out(jax.random.fold_in(part_splits[1], 2), own, number, TOK_DEV, EXPERTS, TOP, CAP, 2))(expert_ids_keys, expert_ids_turns).reshape((TOKENS, TOP))
    gate_scores = jnp.clip(jnp.exp(math.log(1.0) - 2.9957323 * jax.random.uniform(part_splits[2], (TOKENS, TOP), jnp.float32) ** level_of(part_splits[2], (TOKENS, TOP), ((0, 8),), -0.2, 0.2)), 0.05, 1.0)
    gate_weight = bell_draw(key_of[3], (EXPERTS, D, HID), D ** -0.5, 0.09375, ((0, 8), (1, 2)))
    up_weight = bell_draw(key_of[4], (EXPERTS, D, HID), D ** -0.5, 0.09375, ((0, 8), (1, 2)))
    down_weight = bell_draw(key_of[5], (EXPERTS, HID, D), HID ** -0.5, 0.21875, ((0, 8), (2, 2)))
    return {"tokens": tokens, "expert_ids": expert_ids, "gate_scores": gate_scores, "gate_weight": gate_weight, "up_weight": up_weight, "down_weight": down_weight}


def reference(tokens, expert_ids, gate_scores, gate_weight, up_weight, down_weight):
    gate_norm = gate_scores / jnp.sum(gate_scores, axis=1, keepdims=True)
    flat_ids = expert_ids.reshape(-1)
    flat_gates = gate_norm.reshape(-1)
    assigned = flat_ids.shape[0]
    owner_token = jnp.arange(assigned, dtype=jnp.int32) // TOP
    limit_rows = N_EXPERT * CAP
    padded = jnp.concatenate((tokens, jnp.zeros((1, D), tokens.dtype)), axis=0)

    def per_expert(total, inputs):
        expert_index, gate_mat, up_mat, down_mat = inputs
        chosen = flat_ids == expert_index
        running = jnp.cumsum(chosen.astype(jnp.int32)) - 1
        position = jnp.where(chosen, running, limit_rows).astype(jnp.int32)
        source_row = jnp.full((limit_rows + 1,), TOKENS, jnp.int32).at[position].set(owner_token)[:limit_rows]
        weight_row = jnp.zeros((limit_rows + 1,), jnp.float32).at[position].set(flat_gates)[:limit_rows]
        picked = jnp.take(padded, source_row, axis=0)
        pre_gate = jnp.dot(picked, gate_mat, preferred_element_type=jnp.float32)
        pre_up = jnp.dot(picked, up_mat, preferred_element_type=jnp.float32)
        hidden = (jax.nn.silu(pre_gate) * pre_up).astype(jnp.bfloat16)
        expert_out = jnp.dot(hidden, down_mat, preferred_element_type=jnp.float32).astype(jnp.bfloat16)
        total = total.at[source_row].add(weight_row[:, None] * expert_out.astype(jnp.float32))
        return total, None

    start = jnp.zeros((TOKENS + 1, D), jnp.float32)
    expert_range = jnp.arange(EXPERTS, dtype=jnp.int32)
    total, unused_out = lax.scan(per_expert, start, (expert_range, gate_weight, up_weight, down_weight))
    return total[:TOKENS].astype(jnp.bfloat16)
```

```python
import functools

import jax
import jax.numpy as jnp
from jax import lax
from jax.experimental import pallas as pl
from jax.experimental.pallas import tpu as pltpu
from jax.sharding import PartitionSpec as P

MESH = pl.DeviceIdType.MESH
BF16 = jnp.bfloat16
F32 = jnp.float32
TILE = 512


def column_tile(width):
    return TILE if width % TILE == 0 else width


def layer_kernel(n, ring, ids_ref, gates_ref, tok_ref, wg_hbm, wu_hbm, wd_hbm, out_ref,
                 slot_map, gate_map, outgoing, work, back, part, partner_part, wgu, wd, total,
                 w_sem, go_send, go_recv, part_send, part_recv, ret_send, ret_recv):
    me = lax.axis_index("expert")
    other = 1 - lax.axis_index("tensor")
    rows, width = tok_ref.shape
    slots = work.shape[1]
    hid = wd.shape[0]

    def peer_of(j):
        peer, bit = me, 1
        while bit < n:
            peer = peer + bit * ((j // bit) % 2) * (1 - 2 * ((me // bit) % 2))
            bit *= 2
        return peer

    weights = (
        pltpu.make_async_copy(wg_hbm.at[0], wgu.at[:, pl.ds(0, hid)], w_sem.at[0]),
        pltpu.make_async_copy(wu_hbm.at[0], wgu.at[:, pl.ds(hid, hid)], w_sem.at[1]),
        pltpu.make_async_copy(wd_hbm.at[0], wd, w_sem.at[2]),
    )
    for copy in weights:
        copy.start()

    barrier = pltpu.get_barrier_semaphore()

    def greet(j, carry):
        pl.semaphore_signal(barrier, inc=1, device_id={"expert": peer_of(j)}, device_id_type=MESH)
        return carry

    lax.fori_loop(1, n, greet, 0)
    pl.semaphore_signal(barrier, inc=1, device_id={"tensor": other}, device_id_type=MESH)

    ids = ids_ref[...]
    scores = gates_ref[...]
    norm = scores / jnp.sum(scores, axis=0, keepdims=True)
    expert = lax.broadcasted_iota(jnp.int32, (n, rows), 0)
    mask = jnp.zeros((n, rows), F32)
    gate = jnp.zeros((n, rows), F32)
    for k in range(ids.shape[0]):
        hit = ids[k:k + 1, :] == expert
        mask = mask + jnp.where(hit, 1.0, 0.0)
        gate = gate + jnp.where(hit, norm[k:k + 1, :], 0.0)
    earlier = (lax.broadcasted_iota(jnp.int32, (rows, rows), 0)
               < lax.broadcasted_iota(jnp.int32, (rows, rows), 1))
    before = jnp.dot(mask.astype(BF16), jnp.where(earlier, 1.0, 0.0).astype(BF16),
                     preferred_element_type=F32)
    slot_map[...] = jnp.where(mask > 0.5, before, -1.0)
    gate_map[...] = gate

    def chosen(peer):
        place = lax.broadcasted_iota(jnp.int32, (slots, rows), 0).astype(F32)
        return slot_map[pl.ds(peer, 1), :] == place

    def gathered(peer):
        pick = jnp.where(chosen(peer), 1.0, 0.0).astype(BF16)
        return jnp.dot(pick, tok_ref[...], preferred_element_type=F32).astype(BF16)

    def go(j):
        return pltpu.make_async_remote_copy(
            src_ref=outgoing.at[j], dst_ref=work.at[j], send_sem=go_send.at[j], recv_sem=go_recv.at[j],
            device_id={"expert": peer_of(j)}, device_id_type=MESH)

    def ret(j):
        return pltpu.make_async_remote_copy(
            src_ref=work.at[j], dst_ref=back.at[j], send_sem=ret_send.at[j], recv_sem=ret_recv.at[j],
            device_id={"expert": peer_of(j)}, device_id_type=MESH)

    def swap(j):
        r = j % ring
        return pltpu.make_async_remote_copy(
            src_ref=part.at[r], dst_ref=partner_part.at[r], send_sem=part_send.at[r], recv_sem=part_recv.at[r],
            device_id={"tensor": other}, device_id_type=MESH)

    half = n // 2

    def dispatch(j):
        outgoing[j] = gathered(peer_of(j))
        go(j).start()

    outgoing[half] = gathered(peer_of(half))
    pl.semaphore_wait(barrier, n)
    go(half).start()

    def send_pair(j, carry):
        dispatch(j)
        dispatch(half + j)
        return carry

    lax.fori_loop(1, half, send_pair, 0)
    work[0] = gathered(me)

    up_tile = column_tile(2 * hid)
    down_tile = column_tile(width)

    def project(j):
        r = j % ring

        def tile(c, carry):
            cols = pl.ds(pl.multiple_of(c * up_tile, up_tile), up_tile)
            part[r, :, cols] = jnp.dot(work[j], wgu[:, cols], preferred_element_type=F32)
            return carry

        lax.fori_loop(0, 2 * hid // up_tile, tile, 0)
        swap(j).start()

    def finish(j):
        r = j % ring
        swap(j).wait()
        both = part[r] + partner_part[r]
        pre_gate, pre_up = both[:, :hid], both[:, hid:]
        hidden = (pre_gate / (1.0 + jnp.exp(-pre_gate)) * pre_up).astype(BF16)

        for c in range(width // down_tile):
            cols = pl.ds(c * down_tile, down_tile)
            work[j, :, cols] = jnp.dot(hidden, wd[:, cols], preferred_element_type=F32).astype(BF16)

    def step(i, carry):
        @pl.when(i < n)
        def _():
            @pl.when(i == 0)
            def _():
                weights[0].wait()
                weights[1].wait()

            @pl.when(i > 0)
            def _():
                go(i).wait_recv()

            project(i)

        @pl.when(i > 0)
        def _():
            @pl.when(i == 1)
            def _():
                weights[2].wait()

            finish(i - 1)

            @pl.when(i > 1)
            def _():
                ret(i - 1).start()

        return carry

    lax.fori_loop(0, n + 1, step, 0)

    def weighted(j, block):
        peer = peer_of(j)
        share = jnp.where(chosen(peer), gate_map[pl.ds(peer, 1), :], 0.0)
        high = share.astype(BF16)
        low = (share - high.astype(F32)).astype(BF16)
        sides = jnp.concatenate((high, low), axis=1)
        both = lax.dot_general(sides, block, (((0,), (0,)), ((), ())), preferred_element_type=F32)
        return both[:rows] + both[rows:]

    total[...] = weighted(0, work[0])

    def combine(j, carry):
        ret(j).wait_recv()
        total[...] += weighted(j, back[j])
        return carry

    lax.fori_loop(1, n, combine, 0)
    out_ref[...] = total[...].astype(BF16)

    def drain(j, carry):
        go(j).wait_send()
        ret(j).wait_send()
        return carry

    lax.fori_loop(1, n, drain, 0)


def shards(tokens, expert_ids, gate_scores, gate_weight, up_weight, down_weight):
    rows, width = tokens.shape
    top = expert_ids.shape[1]
    n = lax.axis_size("expert")
    hid = gate_weight.shape[2]
    capacity = max(2, min(rows, 5 * rows * top // (4 * n)))
    slots = -(-capacity // 8) * 8
    ring = min(n, 8)
    vmem = pl.BlockSpec(memory_space=pltpu.VMEM)
    hbm = pl.BlockSpec(memory_space=pl.ANY)
    dma = pltpu.SemaphoreType.DMA
    return pl.pallas_call(
        functools.partial(layer_kernel, n, ring),
        out_shape=jax.ShapeDtypeStruct((rows, width), BF16),
        in_specs=[vmem, vmem, vmem, hbm, hbm, hbm],
        out_specs=vmem,
        scratch_shapes=[
            pltpu.VMEM((n, rows), F32),
            pltpu.VMEM((n, rows), F32),
            pltpu.VMEM((n, slots, width), BF16),
            pltpu.VMEM((n, slots, width), BF16),
            pltpu.VMEM((n, slots, width), BF16),
            pltpu.VMEM((ring, slots, 2 * hid), F32),
            pltpu.VMEM((ring, slots, 2 * hid), F32),
            pltpu.VMEM((width, 2 * hid), BF16),
            pltpu.VMEM((hid, width), BF16),
            pltpu.VMEM((rows, width), F32),
            dma((3,)),
            dma((n,)),
            dma((n,)),
            dma((ring,)),
            dma((ring,)),
            dma((n,)),
            dma((n,)),
        ],
        compiler_params=pltpu.CompilerParams(
            collective_id=0, has_side_effects=True, vmem_limit_bytes=58 * 1024 * 1024),
    )(expert_ids.T, gate_scores.T, tokens, gate_weight, up_weight, down_weight)


def solution(mesh):
    in_specs = (
        P(("group", "expert"), "tensor"),
        P(("group", "expert"), None),
        P(("group", "expert"), None),
        P("expert", "tensor", None),
        P("expert", "tensor", None),
        P("expert", None, "tensor"),
    )
    out_specs = P(("group", "expert"), "tensor")
    return jax.shard_map(shards, mesh=mesh, in_specs=in_specs, out_specs=out_specs, check_vma=False)
```

```python
import functools

import jax
import jax.numpy as jnp
from jax import lax
from jax.experimental import pallas as pl
from jax.experimental.pallas import tpu as pltpu
from jax.sharding import PartitionSpec as P

MESH = pl.DeviceIdType.MESH
BF16 = jnp.bfloat16
F32 = jnp.float32
TILE = 512


def column_tile(width):
    return TILE if width % TILE == 0 else width


def layer_kernel(n, chunks, ring, ids_ref, gates_ref, tok_ref, wg_hbm, wu_hbm, wd_hbm, out_ref,
                 own_map, far_out_map, far_map, far_tok, outgoing, work, back, part, partner_part,
                 flat, wgu, wd, total, sum_out, sum_in,
                 w_sem, map_sem, far_send, far_recv, go_send, go_recv, part_send, part_recv,
                 ret_send, ret_recv, sum_send, sum_recv, free_sem):
    me = lax.axis_index("expert")
    other = 1 - lax.axis_index("tensor")
    rows, width = tok_ref.shape
    near, slots = work.shape[1], work.shape[2]
    hid = wd.shape[0]
    deep = near * slots
    span = rows // chunks
    sets = 1 + chunks
    far = near + me - 2 * near * (me // near)

    def peer_of(q):
        peer, bit = me, 1
        while bit < near:
            peer = peer + bit * ((q // bit) % 2) * (1 - 2 * ((me // bit) % 2))
            bit *= 2
        return peer

    def send(src, dst, send_sem, recv_sem, to):
        return pltpu.make_async_remote_copy(
            src_ref=src, dst_ref=dst, send_sem=send_sem, recv_sem=recv_sem,
            device_id=to, device_id_type=MESH)

    def go(s, q):
        return send(outgoing.at[s, q], work.at[s, q], go_send.at[s, q], go_recv.at[s, q], {"expert": peer_of(q)})

    def ret(s, q):
        return send(work.at[s, q], back.at[s, q], ret_send.at[s, q], ret_recv.at[s, q], {"expert": peer_of(q)})

    def swap(s):
        r = s % ring
        return send(part.at[r], partner_part.at[r], part_send.at[r], part_recv.at[r], {"tensor": other})

    def cross(r):
        return send(tok_ref.at[pl.ds(r * span, span)], far_tok.at[r], far_send.at[r], far_recv.at[r], {"expert": far})

    def cross_back(r):
        return send(sum_out.at[r], sum_in.at[r], sum_send.at[r], sum_recv.at[r], {"expert": far})

    maps = send(far_out_map, far_map, map_sem.at[0], map_sem.at[1], {"expert": far})

    weights = (
        pltpu.make_async_copy(wg_hbm.at[0], wgu.at[:, pl.ds(0, hid)], w_sem.at[0]),
        pltpu.make_async_copy(wu_hbm.at[0], wgu.at[:, pl.ds(hid, hid)], w_sem.at[1]),
        pltpu.make_async_copy(wd_hbm.at[0], wd, w_sem.at[2]),
    )
    barrier = pltpu.get_barrier_semaphore()
    pl.semaphore_signal(barrier, inc=1, device_id={"expert": far}, device_id_type=MESH)

    def greet(q, carry):
        pl.semaphore_signal(barrier, inc=1, device_id={"expert": peer_of(q)}, device_id_type=MESH)
        return carry

    lax.fori_loop(1, near, greet, 0)
    pl.semaphore_signal(barrier, inc=1, device_id={"tensor": other}, device_id_type=MESH)
    for copy in weights:
        copy.start()
    pl.semaphore_wait(barrier, near + 1)
    cross(0).start()

    ids = ids_ref[...]
    scores = gates_ref[...]
    norm = scores / jnp.sum(scores, axis=0, keepdims=True)
    expert = lax.broadcasted_iota(jnp.int32, (n, rows), 0)
    mask = jnp.zeros((n, rows), F32)
    gate = jnp.zeros((n, rows), F32)
    for k in range(ids.shape[0]):
        hit = ids[k:k + 1, :] == expert
        mask = mask + jnp.where(hit, 1.0, 0.0)
        gate = gate + jnp.where(hit, norm[k:k + 1, :], 0.0)
    first = lax.broadcasted_iota(jnp.int32, (rows, rows), 0)
    second = lax.broadcasted_iota(jnp.int32, (rows, rows), 1)
    earlier = jnp.where(first < second, 1.0, 0.0)

    def slot_of(ahead):
        before = jnp.dot(mask.astype(BF16), ahead.astype(BF16), preferred_element_type=F32)
        return jnp.where(mask > 0.5, before, -1.0)

    own_map[0:n, :] = slot_of(earlier)
    own_map[n:2 * n, :] = gate
    for r in range(1, chunks):
        earlier = jnp.where((first < r * span) & (second >= r * span), 0.0, earlier)
    far_out_map[0:n, :] = slot_of(earlier)
    far_out_map[n:2 * n, :] = gate
    maps.start()

    def row_of(table, index, lo, count):
        line = table[pl.ds(index, 1), :]
        return line if count == rows else line[:, lo:lo + count]

    def chosen(table, peer, lo, count):
        place = lax.broadcasted_iota(jnp.int32, (slots, count), 0).astype(F32)
        return row_of(table, peer, lo, count) == place

    def scatter_out(s, table, lo, count, source):
        pick = jnp.concatenate(
            [jnp.where(chosen(table, peer_of(q), lo, count), 1.0, 0.0) for q in range(near)], axis=0).astype(BF16)
        for c in range(width // column_tile(width)):
            cols = slice(c * column_tile(width), (c + 1) * column_tile(width))
            moved = jnp.dot(pick, source[:, cols], preferred_element_type=F32)
            moved = moved.reshape(near, slots, column_tile(width)).astype(BF16)
            work[s, 0, :, cols] = moved[0]
            for q in range(1, near):
                outgoing[s, q, :, cols] = moved[q]

        def start(q, carry):
            go(s, q).start()
            return carry

        lax.fori_loop(1, near, start, 0)

    def flatten(source, s):
        for c in range(width // column_tile(width)):
            cols = slice(c * column_tile(width), (c + 1) * column_tile(width))
            flat[:, cols] = source[s, :, :, cols].astype(F32).reshape(deep, column_tile(width)).astype(BF16)

    def project(s):
        def arrive(q, carry):
            go(s, q).wait_recv()
            return carry

        lax.fori_loop(1, near, arrive, 0)
        flatten(work, s)
        r = s % ring
        if ring < sets and s > 0:
            pl.semaphore_wait(free_sem, 1)
        up_tile = column_tile(2 * hid)

        def tile(c, carry):
            cols = pl.ds(pl.multiple_of(c * up_tile, up_tile), up_tile)
            part[r, :, cols] = jnp.dot(flat[...], wgu[:, cols], preferred_element_type=F32)
            return carry

        lax.fori_loop(0, 2 * hid // up_tile, tile, 0)
        swap(s).start()

    def finish(s):
        r = s % ring
        swap(s).wait()
        pre_gate = part[r, :, :hid] + partner_part[r, :, :hid]
        pre_up = part[r, :, hid:] + partner_part[r, :, hid:]
        hidden = (pre_gate / (1.0 + jnp.exp(-pre_gate)) * pre_up).astype(BF16)
        if ring < sets and s < sets - 1:
            pl.semaphore_signal(free_sem, inc=1, device_id={"tensor": other}, device_id_type=MESH)
        for c in range(width // column_tile(width)):
            cols = slice(c * column_tile(width), (c + 1) * column_tile(width))
            result = jnp.dot(hidden, wd[:, cols], preferred_element_type=F32)
            result = result.reshape(near, slots, column_tile(width)).astype(BF16)
            back[s, 0, :, cols] = result[0]
            for q in range(1, near):
                work[s, q, :, cols] = result[q]

        def start(q, carry):
            ret(s, q).start()
            return carry

        lax.fori_loop(1, near, start, 0)

    def weighted(s, table, lo, count):
        shares = jnp.concatenate(
            [jnp.where(chosen(table, peer_of(q), lo, count), row_of(table, n + peer_of(q), lo, count), 0.0)
             for q in range(near)], axis=0)
        high = shares.astype(BF16)
        low = (shares - high.astype(F32)).astype(BF16)
        sides = jnp.concatenate((high, low), axis=1)

        def arrive(q, carry):
            ret(s, q).wait_recv()
            return carry

        lax.fori_loop(1, near, arrive, 0)
        flatten(back, s)
        both = lax.dot_general(sides, flat[...], (((0,), (0,)), ((), ())), preferred_element_type=F32)
        return both[:count] + both[count:]

    def relay(r):
        cross(r).wait_recv()
        scatter_out(1 + r, far_map, r * span, span, far_tok.at[r])

    def answer(r):
        sum_out[r] = weighted(1 + r, far_map, r * span, span).astype(BF16)
        cross_back(r).start()

    scatter_out(0, own_map, 0, rows, tok_ref)
    weights[0].wait()
    weights[1].wait()
    project(0)
    for r in range(1, chunks):
        cross(r).start()
    weights[2].wait()
    finish(0)
    maps.wait()
    relay(0)
    project(1)
    finish(1)
    for r in range(1, chunks):
        relay(r)
        answer(r - 1)
        project(1 + r)
        finish(1 + r)
    total[...] = weighted(0, own_map, 0, rows)
    answer(chunks - 1)
    for r in range(chunks):
        cross_back(r).wait_recv()
        lines = slice(r * span, (r + 1) * span)
        out_ref[lines, :] = (total[lines, :] + sum_in[r].astype(F32)).astype(BF16)

    for r in range(chunks):
        cross(r).wait_send()
        cross_back(r).wait_send()
    for s in range(sets):
        def drain(q, carry):
            go(s, q).wait_send()
            ret(s, q).wait_send()
            return carry

        lax.fori_loop(1, near, drain, 0)


def shards(tokens, expert_ids, gate_scores, gate_weight, up_weight, down_weight):
    rows, width = tokens.shape
    top = expert_ids.shape[1]
    n = lax.axis_size("expert")
    hid = gate_weight.shape[2]
    capacity = max(2, min(rows, 5 * rows * top // (4 * n)))
    slots = -(-capacity // 8) * 8
    near = n // 2
    chunks = 2 if n <= 8 else 1
    sets = 1 + chunks
    ring = sets if n <= 8 else 1
    span = rows // chunks
    vmem = pl.BlockSpec(memory_space=pltpu.VMEM)
    hbm = pl.BlockSpec(memory_space=pl.ANY)
    dma = pltpu.SemaphoreType.DMA
    return pl.pallas_call(
        functools.partial(layer_kernel, n, chunks, ring),
        out_shape=jax.ShapeDtypeStruct((rows, width), BF16),
        in_specs=[vmem, vmem, vmem, hbm, hbm, hbm],
        out_specs=vmem,
        scratch_shapes=[
            pltpu.VMEM((2 * n, rows), F32),
            pltpu.VMEM((2 * n, rows), F32),
            pltpu.VMEM((2 * n, rows), F32),
            pltpu.VMEM((chunks, span, width), BF16),
            pltpu.VMEM((sets, near, slots, width), BF16),
            pltpu.VMEM((sets, near, slots, width), BF16),
            pltpu.VMEM((sets, near, slots, width), BF16),
            pltpu.VMEM((ring, near * slots, 2 * hid), F32),
            pltpu.VMEM((ring, near * slots, 2 * hid), F32),
            pltpu.VMEM((near * slots, width), BF16),
            pltpu.VMEM((width, 2 * hid), BF16),
            pltpu.VMEM((hid, width), BF16),
            pltpu.VMEM((rows, width), F32),
            pltpu.VMEM((chunks, span, width), BF16),
            pltpu.VMEM((chunks, span, width), BF16),
            dma((3,)),
            dma((2,)),
            dma((chunks,)),
            dma((chunks,)),
            dma((sets, near)),
            dma((sets, near)),
            dma((ring,)),
            dma((ring,)),
            dma((sets, near)),
            dma((sets, near)),
            dma((chunks,)),
            dma((chunks,)),
            pltpu.SemaphoreType.REGULAR,
        ],
        compiler_params=pltpu.CompilerParams(
            collective_id=0, has_side_effects=True, vmem_limit_bytes=60 * 1024 * 1024),
    )(expert_ids.T, gate_scores.T, tokens, gate_weight, up_weight, down_weight)


def solution(mesh):
    in_specs = (
        P(("group", "expert"), "tensor"),
        P(("group", "expert"), None),
        P(("group", "expert"), None),
        P("expert", "tensor", None),
        P("expert", "tensor", None),
        P("expert", None, "tensor"),
    )
    out_specs = P(("group", "expert"), "tensor")
    return jax.shard_map(shards, mesh=mesh, in_specs=in_specs, out_specs=out_specs, check_vma=False)
```
